512 devices in a mesh: group: 32 (over z_hi, y, core), head: 16 (over x, z_lo).
Axes of the slice: x: 4, y: 4, z: 16 (z_hi: 4, z_lo: 4; z = z_hi * 4 + z_lo), core: 2. Of those that a mesh axis runs over, the one named last changes fastest.
Arguments:
- queries: bfloat16 [1024, 4, 128, 576], P('group', None, 'head'), may hold values from -48 to 48
- new_latent: bfloat16 [1024, 4, 576], P('group'), may hold values from -4 to 4
- own_cache: bfloat16 [1024, 32, 576], P('group'), may hold values from -4 to 4
- prompt_pool: bfloat16 [32, 32, 64, 576], P('group', 'head'), may hold values from -4 to 4
- uv_weight: bfloat16 [128, 512, 128], P('head'), may hold values from -0.25 to 0.25
- owner: int32 [32], replicated, may hold values from 0 to 31, as said below
- route: int32 [32], P('group'), may hold values from 0 to 1
- prompt_len: int32 [1024], P('group'), may hold values from 1 to 2048, as said below
- page_table: int32 [32], replicated, may hold values from 0 to 31, each once
Outputs:
- attended: bfloat16 [1024, 4, 16384], P('group', None, 'head')
The draws below stay inside these ranges and needn't reach their ends.
Inputs may be any that keep to these rules, and one draw needn't show every extreme that they name: `owner`: each of the 32 numbers appears once. `prompt_len`: the first request of every group reads the whole prompt. `page_table`: each of the 32 slots appears once.
All inputs are finite; a program needn't handle non-finite values.
Results may differ from the reference program's by a relative error of at most 0.0065.
Values may be sent and summed in bfloat16 or wider, within the bound.
No kernel may reach another device: no remote copies, remote signals or barrier semaphores. Data moves between devices by JAX's collectives and lax.ppermute only.
A program may use at most 64 MiB of HBM per device.

```python
import jax
import jax.numpy as jnp
from jax import lax

HEADS = 128
KV_RANK = 512
VHEAD = 128
LAT = 576
REQ = 32
STEPS = 4
OWN = 32
PAGE = 64
PROMPT = 2048
PAGES = 32
GROUPS = 32


def fresh_latent(key):
    common = jax.random.normal(key, (GROUPS * REQ, STEPS, LAT), jnp.float32)
    return jnp.clip(common, -4.0, 4.0)


def group_order(key):
    return jax.random.permutation(key, GROUPS).astype(jnp.int32)


def draw_owner(key, part):
    order = group_order(key)
    return order


def draw_route(key, part):
    order = group_order(key)
    key = jax.random.fold_in(key, 13)
    group_ids = jnp.arange(GROUPS, dtype=jnp.int32)
    root = jnp.sum(jnp.where(order == 0, group_ids, 0)).astype(jnp.int32)
    served = jax.random.randint(key, (GROUPS,), 0, 2, jnp.int32)
    forced = (group_ids == (root + 1) % GROUPS) | (group_ids == (root + GROUPS - 1) % GROUPS) | (group_ids == (root + GROUPS // 2) % GROUPS)
    return jnp.where(forced, 1, served).astype(jnp.int32)


def draw_new_latent(key, part):
    common = fresh_latent(key)
    return common.astype(jnp.bfloat16)


def draw_prompt_pool(key, part):
    key = jax.random.fold_in(key, 7)
    extent = (GROUPS, PAGES, PAGE, LAT)
    values = jnp.clip(jax.random.normal(key, extent, jnp.float32), -4.0, 4.0)
    return values.astype(jnp.bfloat16)


def draw_queries(key, part):
    key = jax.random.fold_in(key, 5)
    extent = (GROUPS * REQ, STEPS, HEADS, LAT)
    values = jnp.clip(jax.random.normal(key, extent, jnp.float32), -4.0, 4.0)
    return values.astype(jnp.bfloat16)


def draw_prompt_len(key, part):
    key = jax.random.fold_in(key, 11)
    lengths = jax.random.randint(key, (GROUPS * REQ,), 1, PROMPT + 1, jnp.int32)
    firsts = jnp.arange(GROUPS * REQ) % REQ == 0
    return jnp.where(firsts, PROMPT, lengths).astype(jnp.int32)


def level_of(stream_key, shape, cuts, low, largest):
    level, own = 1.0, jax.random.fold_in(stream_key, 6)
    for axis_at, blocks in cuts:
        draws = jnp.exp(jax.random.uniform(jax.random.fold_in(own, axis_at), (blocks,), jnp.float32, low / len(cuts), largest / len(cuts)))
        level = level * jnp.repeat(draws, shape[axis_at] // blocks).reshape([-1 if axis == axis_at else 1 for axis in range(len(shape))])
    return level


def gaussian(rng, shape, spread, bound, pieces=(), kind=jnp.bfloat16):
    entries = jax.random.normal(rng, shape, jnp.float32) * spread
    if len(pieces) > 0:
        entries = level_of(rng, shape, pieces, -0.22, 0.18) * entries
    return jnp.clip(entries, min=-bound, max=bound).astype(kind)


def setup_inputs(seed: int = 0) -> dict:
    splits = jax.random.split(jax.random.key(seed), 10)
    return {
        "queries": draw_queries(jax.random.fold_in(splits[9], 71), 0),
        "new_latent": draw_new_latent(jax.random.fold_in(splits[9], 71), 0),
        "own_cache": gaussian(splits[2], (GROUPS * REQ, OWN, LAT), 1.0, 4.0, ((0, 32),)),
        "prompt_pool": draw_prompt_pool(jax.random.fold_in(splits[9], 71), 0),
        "uv_weight": gaussian(splits[4], (HEADS, KV_RANK, VHEAD), KV_RANK ** -0.5, 0.25, ((0, 16),)),
        "owner": draw_owner(jax.random.fold_in(splits[9], 71), 0),
        "route": draw_route(jax.random.fold_in(splits[9], 71), 0),
        "prompt_len": draw_prompt_len(jax.random.fold_in(splits[9], 71), 0),
        "page_table": jax.random.permutation(splits[8], PAGES).astype(jnp.int32),
    }


softmax_scale = 192.0 ** -0.5
lowest_score = -1.0e30


def reference(queries, new_latent, own_cache, prompt_pool, uv_weight, owner, route, prompt_len, page_table):
    group_ids = jnp.arange(GROUPS, dtype=jnp.int32)
    root = jnp.sum(jnp.where(owner == 0, group_ids, 0)).astype(jnp.int32)
    owned = lax.dynamic_index_in_dim(prompt_pool, root, 0, keepdims=False)
    prompt_keys = jnp.take(owned, page_table, axis=0).reshape(PROMPT, LAT).astype(jnp.float32)
    uv_float = uv_weight.astype(jnp.float32)
    positions = jnp.arange(PROMPT, dtype=jnp.int32)
    steps_seen = jnp.arange(STEPS)[None, :] <= jnp.arange(STEPS)[:, None]
    local_seen = jnp.concatenate([jnp.ones((STEPS, OWN), bool), steps_seen], axis=1)[None, :, None, :]

    def one_group(inputs):
        group_queries, group_new, group_own, active, lengths = inputs
        query_float = group_queries.astype(jnp.float32)
        local_keys = jnp.concatenate([group_own, group_new], axis=1).astype(jnp.float32)
        prompt_scores = jnp.einsum('rthc,kc->rthk', query_float, prompt_keys) * softmax_scale
        local_scores = jnp.einsum('rthc,rkc->rthk', query_float, local_keys) * softmax_scale
        prompt_seen = ((positions[None, :] < lengths[:, None]) & (active > 0))[:, None, None, :]
        peak = jnp.maximum(jnp.max(jnp.where(prompt_seen, prompt_scores, lowest_score), axis=-1),
                           jnp.max(jnp.where(local_seen, local_scores, lowest_score), axis=-1))[..., None]
        prompt_exp = jnp.where(prompt_seen, jnp.exp(prompt_scores - peak), 0.0)
        local_exp = jnp.where(local_seen, jnp.exp(local_scores - peak), 0.0)
        denominator = jnp.sum(prompt_exp, axis=-1) + jnp.sum(local_exp, axis=-1)
        rounded_prompt = lax.optimization_barrier(prompt_exp.astype(jnp.bfloat16)).astype(jnp.float32)
        rounded_local = lax.optimization_barrier(local_exp.astype(jnp.bfloat16)).astype(jnp.float32)
        weighted = jnp.einsum('rthk,kc->rthc', rounded_prompt, prompt_keys[:, :KV_RANK])
        weighted = weighted + jnp.einsum('rthk,rkc->rthc', rounded_local, local_keys[:, :, :KV_RANK])
        latent_out = lax.optimization_barrier((weighted / denominator[..., None]).astype(jnp.bfloat16)).astype(jnp.float32)
        attended = jnp.einsum('rthc,hcv->rthv', latent_out, uv_float)
        return attended.reshape(REQ, STEPS, HEADS * VHEAD).astype(jnp.bfloat16)

    outputs = lax.map(one_group, (queries.reshape(GROUPS, REQ, STEPS, HEADS, LAT),
                                  new_latent.reshape(GROUPS, REQ, STEPS, LAT),
                                  own_cache.reshape(GROUPS, REQ, OWN, LAT),
                                  route,
                                  prompt_len.reshape(GROUPS, REQ)))
    return outputs.reshape(GROUPS * REQ, STEPS, HEADS * VHEAD)
```

```python
import functools

import jax
import jax.numpy as jnp
from jax import lax
from jax.experimental import pallas as pl
from jax.experimental.pallas import tpu as pltpu
from jax.sharding import Mesh, PartitionSpec as P
import numpy as np

softmax_scale = 192.0 ** (-0.5)
lowest_score = -1e30
log2_scale = softmax_scale * 1.4426950408889634

axis_names = ("zh", "y", "c", "x", "zl")
axis_sizes = (4, 4, 2, 4, 4)
group_axes = ("zh", "y", "c")
head_axes = ("x", "zl")


def moves(change):
    pairs = []
    for index, place in enumerate(np.ndindex(*axis_sizes)):
        pairs.append((index, int(np.ravel_multi_index(change(*place), axis_sizes))))
    return pairs


def shift_high(steps):
    return moves(lambda zh, y, c, x, zl: ((zh + steps) % 4, y, c, x, zl))


def gathered(value, axes, count):
    tiled = jnp.broadcast_to(value[None], (count,) + value.shape)
    return lax.all_to_all(tiled, axes, 0, 0, tiled=True)


def keys_stats(query, keys, places, lens_ref, first_request, rows_per_request):
    scores = lax.dot_general(
        query, keys, (((1,), (1,)), ((), ())), preferred_element_type=jnp.float32
    )
    rows, key_count = scores.shape
    parts = []
    for number in range(rows // rows_per_request):
        seen = places < lens_ref[first_request + number]
        part = scores[number * rows_per_request : (number + 1) * rows_per_request]
        part = part.reshape(rows_per_request // 8, 8, key_count)
        parts.append(jnp.where(seen[None], part, lowest_score).reshape(-1, key_count))
    scores = jnp.concatenate(parts, axis=0)
    maxima = jnp.max(scores, axis=1, keepdims=True)
    expons = jnp.exp2(scores * log2_scale - maxima * log2_scale)
    sums = jnp.sum(expons, axis=1, keepdims=True)
    return maxima, sums, expons.astype(jnp.bfloat16)


def first_kernel(rank_dim, rows_per_request, lens_ref, query_ref, keys_ref, places_ref,
                 max_ref, sum_ref, acc_ref):
    block = query_ref.shape[0]
    start = pl.program_id(0) * (block // rows_per_request)
    maxima, sums, weights = keys_stats(
        query_ref[...], keys_ref[...], places_ref[...], lens_ref, start, rows_per_request
    )
    acc_ref[...] = jnp.dot(
        weights, keys_ref[:, :rank_dim], preferred_element_type=jnp.float32
    )
    max_ref[...] = jnp.broadcast_to(maxima, max_ref.shape)
    sum_ref[...] = jnp.broadcast_to(sums, sum_ref.shape)


def last_kernel(rank_dim, rows_per_request, heads, lens_ref, query_ref, keys_ref, places_ref,
                max_ref, sum_ref, acc_ref, local_max_ref, local_sum_ref, local_acc_ref,
                uv_ref, out_ref, latent_ref):
    step = pl.program_id(0)
    block = query_ref.shape[0]
    start = step * (block // rows_per_request)
    maxima, sums, weights = keys_stats(
        query_ref[...], keys_ref[...], places_ref[...], lens_ref, start, rows_per_request
    )
    weighted = jnp.dot(
        weights, keys_ref[:, :rank_dim], preferred_element_type=jnp.float32
    )
    first_max = max_ref[:, :1]
    local_max = local_max_ref[...]
    peak = jnp.maximum(jnp.maximum(maxima, first_max), local_max)
    factor = jnp.exp2((maxima - peak) * log2_scale)
    first_factor = jnp.exp2((first_max - peak) * log2_scale)
    local_factor = jnp.exp2((local_max - peak) * log2_scale)
    total = sums * factor + sum_ref[:, :1] * first_factor + local_sum_ref[...] * local_factor
    inverse = 1.0 / total
    latent = (
        weighted * (factor * inverse)
        + acc_ref[...] * (first_factor * inverse)
        + local_acc_ref[...] * (local_factor * inverse)
    )
    latent = latent.astype(jnp.bfloat16).astype(jnp.float32)
    at = pl.ds(pl.multiple_of(step * block, block), block)
    for part in range(latent_ref.shape[0]):
        latent_ref[part, at, :] = latent[:, part * 128 : (part + 1) * 128]

    @pl.when(step == pl.num_programs(0) - 1)
    def project():
        tokens = out_ref.shape[0]
        vhead = uv_ref.shape[2]
        for head in range(heads):
            rows = jnp.concatenate(
                [
                    latent_ref[part, pl.ds(head, tokens, stride=heads), :].astype(jnp.bfloat16)
                    for part in range(latent_ref.shape[0])
                ],
                axis=1,
            )
            out_ref[:, head * vhead : (head + 1) * vhead] = jnp.dot(
                rows, uv_ref[head], preferred_element_type=jnp.float32
            ).astype(jnp.bfloat16)


def body(
    queries, new_latent, own_cache, prompt_pool, uv_weight, owner, route, prompt_len, page_table
):
    requests, num_steps, head_dev, latent = queries.shape
    rank_dim = uv_weight.shape[1]
    vhead_dim = uv_weight.shape[2]
    own_pages, page_len = prompt_pool.shape[1:3]
    num_pages = page_table.shape[0]
    row_count = requests * num_steps * head_dev
    rows_per_request = num_steps * head_dev
    query_rows = queries.reshape(row_count, latent)
    query_block = queries.reshape(requests, rows_per_request, latent)

    group_ids = jnp.arange(owner.shape[0], dtype=jnp.int32)
    root = jnp.sum(jnp.where(owner == 0, group_ids, 0))
    root_high = root // 8
    root_piece = root % 8

    pieces = prompt_pool.reshape(8, own_pages * page_len // 8, latent)
    pieces = lax.all_to_all(pieces, ("y", "c"), 0, 0, tiled=True)
    piece = lax.dynamic_index_in_dim(pieces, root_piece, 0, keepdims=False)
    up = lax.ppermute(piece, axis_names, shift_high(1))
    down = lax.ppermute(piece, axis_names, shift_high(3))
    across = lax.ppermute(piece, axis_names, shift_high(2))
    apart = (lax.axis_index("zh") - root_high) % 4
    piece = jnp.where(
        apart == 0, piece, jnp.where(apart == 1, up, jnp.where(apart == 3, down, across))
    )
    run = gathered(piece, "zl", 4)
    half = gathered(run.reshape(-1, latent), ("x", "y"), 16)
    other = lax.ppermute(half, "c", [(0, 1), (1, 0)]).reshape(-1, latent)
    half = half.reshape(-1, latent)

    own_scores = jnp.einsum(
        "rqc,rkc->rqk", query_block, own_cache, preferred_element_type=jnp.float32
    )
    new_scores = jnp.einsum(
        "rqc,rkc->rqk", query_block, new_latent, preferred_element_type=jnp.float32
    )
    step_of_row = jnp.arange(rows_per_request, dtype=jnp.int32) // head_dev
    new_seen = jnp.arange(num_steps, dtype=jnp.int32)[None, :] <= step_of_row[:, None]
    new_scores = jnp.where(new_seen[None], new_scores, lowest_score)
    local_max = jnp.maximum(jnp.max(own_scores, axis=-1), jnp.max(new_scores, axis=-1))
    own_exp = jnp.exp2((own_scores - local_max[..., None]) * log2_scale)
    new_exp = jnp.exp2((new_scores - local_max[..., None]) * log2_scale)
    local_sums = jnp.sum(own_exp, axis=-1) + jnp.sum(new_exp, axis=-1)
    local_weighted = jnp.einsum(
        "rqk,rkc->rqc", own_exp.astype(jnp.bfloat16), own_cache[:, :, :rank_dim],
        preferred_element_type=jnp.float32,
    ) + jnp.einsum(
        "rqk,rkc->rqc", new_exp.astype(jnp.bfloat16), new_latent[:, :, :rank_dim],
        preferred_element_type=jnp.float32,
    )
    local_max = local_max.reshape(row_count, 1)
    local_sums = local_sums.reshape(row_count, 1)
    local_weighted = local_weighted.reshape(row_count, rank_dim)

    slots = jnp.arange(num_pages, dtype=jnp.int32)
    matches = (page_table[:, None] == slots[None, :]).astype(jnp.int32)
    logical = jnp.sum(matches * slots[:, None], axis=0)
    core = lax.axis_index("c")
    piece_rows = own_pages * page_len // 8
    firsts = jnp.broadcast_to(
        logical.reshape(4, 1, 4, own_pages, 1) * page_len, (4, 1, 4, own_pages, 1)
    )
    firsts = jnp.moveaxis(firsts, 3, 1).reshape(4, own_pages, 1, 4, 1)
    within = (
        (jnp.arange(2, dtype=jnp.int32) * 2)[None, None, :, None, None] * piece_rows
        + jnp.arange(piece_rows, dtype=jnp.int32)[None, None, None, None, :]
    )
    places = (firsts + within).reshape(1, -1)
    key_count = places.shape[1]
    places = jnp.broadcast_to(places, (8, key_count))
    own_places = places + core * piece_rows
    other_places = places + (1 - core) * piece_rows
    lens = jnp.where(route[0] > 0, prompt_len, 0)

    block = 256
    steps = row_count // block
    whole = lambda shape: pl.BlockSpec(shape, lambda i, lens: (0,) * len(shape))
    rows = lambda width: pl.BlockSpec((block, width), lambda i, lens: (i, 0))
    cost = pl.CostEstimate(
        flops=2 * row_count * key_count * (latent + rank_dim),
        bytes_accessed=2 * (row_count + key_count) * latent + 4 * row_count * rank_dim,
        transcendentals=row_count * key_count,
    )
    params = pltpu.CompilerParams(vmem_limit_bytes=24 * 1024 * 1024)
    first = pl.pallas_call(
        functools.partial(first_kernel, rank_dim, rows_per_request),
        grid_spec=pltpu.PrefetchScalarGridSpec(
            num_scalar_prefetch=1,
            grid=(steps,),
            in_specs=[rows(latent), whole((key_count, latent)), whole((8, key_count))],
            out_specs=[rows(128), rows(128), rows(rank_dim)],
        ),
        out_shape=[
            jax.ShapeDtypeStruct((row_count, 128), jnp.float32),
            jax.ShapeDtypeStruct((row_count, 128), jnp.float32),
            jax.ShapeDtypeStruct((row_count, rank_dim), jnp.float32),
        ],
        compiler_params=params,
        cost_estimate=cost,
    )
    first_max, first_sum, first_acc = first(lens, query_rows, half, own_places)
    last = pl.pallas_call(
        functools.partial(last_kernel, rank_dim, rows_per_request, head_dev),
        grid_spec=pltpu.PrefetchScalarGridSpec(
            num_scalar_prefetch=1,
            grid=(steps,),
            in_specs=[
                rows(latent), whole((key_count, latent)), whole((8, key_count)),
                rows(128), rows(128), rows(rank_dim), rows(1), rows(1), rows(rank_dim),
                whole(uv_weight.shape),
            ],
            out_specs=whole((row_count // head_dev, head_dev * vhead_dim)),
            scratch_shapes=[pltpu.VMEM((rank_dim // 128, row_count, 128), jnp.float32)],
        ),
        out_shape=jax.ShapeDtypeStruct((row_count // head_dev, head_dev * vhead_dim), jnp.bfloat16),
        compiler_params=params,
        cost_estimate=cost,
    )
    attended = last(
        lens, query_rows, other, other_places, first_max, first_sum, first_acc,
        local_max, local_sums, local_weighted, uv_weight,
    )
    return attended.reshape(requests, num_steps, head_dev * vhead_dim)


def solution(mesh):
    fine = Mesh(mesh.devices.reshape(axis_sizes), axis_names)
    placed = (
        P(group_axes, None, head_axes, None),
        P(group_axes, None, None),
        P(group_axes, None, None),
        P(group_axes, head_axes, None, None),
        P(head_axes, None, None),
        P(),
        P(group_axes),
        P(group_axes),
        P(),
    )
    return jax.shard_map(
        body, mesh=fine, in_specs=placed, out_specs=P(group_axes, None, head_axes), check_vma=False
    )
```

```python
import functools

import jax
import jax.numpy as jnp
from jax import lax
from jax.experimental import pallas as pl
from jax.experimental.pallas import tpu as pltpu
from jax.sharding import Mesh, PartitionSpec as P

softmax_scale = 192.0 ** (-0.5)
lowest_score = -1e30
log2_scale = softmax_scale * 1.4426950408889634

axis_names = ("zh", "y", "c", "x", "zl")
axis_sizes = (4, 4, 2, 4, 4)
group_axes = ("zh", "y", "c")
head_axes = ("x", "zl")


def from_high(high, piece):
    place = lax.axis_index("zh")
    up, down, across = (high + 1) % 4, (high + 3) % 4, (high + 2) % 4
    above = lax.ppermute(piece, "zh", [(high, up)])
    below = lax.ppermute(piece, "zh", [(high, down)])
    beyond = lax.ppermute(above, "zh", [(up, across)])
    result = jnp.where(place == up, above, piece)
    result = jnp.where(place == down, below, result)
    return jnp.where(place == across, beyond, result)


def gathered(value, axes, count):
    tiled = jnp.broadcast_to(value[None], (count,) + value.shape)
    return lax.all_to_all(tiled, axes, 0, 0, tiled=True)


def scores_of(query, keys):
    return lax.dot_general(
        query, keys, (((1,), (1,)), ((), ())), preferred_element_type=jnp.float32
    )


def read_stats(stats_ref, at):
    return stats_ref[at, 0:1], stats_ref[at, 1:2]


def write_stats(stats_ref, at, maxima, sums):
    rows = maxima.shape[0]
    lane = lax.broadcasted_iota(jnp.int32, (rows, stats_ref.shape[1]), 1)
    stats_ref[at, :] = jnp.where(lane == 0, maxima, sums)


def write_places(page_len, piece_rows, table_ref, places_ref):
    shape = (8, places_ref.shape[1])
    lane = lax.broadcasted_iota(jnp.int32, shape, 1)
    offset = lane % piece_rows
    low = lane // piece_rows % 4
    lower = lane // (piece_rows * 4) % 2
    page = lane // (piece_rows * 8) % 2
    slot = (lane // (piece_rows * 16) * 4 + low) * 2 + page
    places = lower * (2 * piece_rows) + offset
    for logical in range(table_ref.shape[0]):
        places += jnp.where(slot == table_ref[logical], logical * page_len, 0)
    core = lax.axis_index("c")
    places_ref[0:8, :] = places + core * piece_rows
    places_ref[8:16, :] = places + (1 - core) * piece_rows


def local_kernel(heads, steps, block, page_len, piece_rows, table_ref, query_ref, own_ref, new_ref,
                 stats_ref, acc_ref, places_ref):
    write_places(page_len, piece_rows, table_ref, places_ref)
    rows = query_ref.shape[0]
    rank_dim = acc_ref.shape[1]
    per_request = heads * steps
    requests = rows // per_request
    own_len = own_ref.shape[0] // requests
    per_block = block // per_request
    row = lax.broadcasted_iota(jnp.int32, (block, per_block * own_len), 0)
    key = lax.broadcasted_iota(jnp.int32, (block, per_block * own_len), 1)
    own_seen = row // per_request == key // own_len
    row = lax.broadcasted_iota(jnp.int32, (block, per_block * steps), 0)
    key = lax.broadcasted_iota(jnp.int32, (block, per_block * steps), 1)
    new_seen = (row // per_request == key // steps) & (
        key % steps <= (row % per_request) // heads
    )
    for number in range(rows // block):
        at = slice(number * block, (number + 1) * block)
        query = query_ref[at, :]
        own = own_ref[number * per_block * own_len : (number + 1) * per_block * own_len, :]
        new = new_ref[number * per_block * steps : (number + 1) * per_block * steps, :]
        own_scores = jnp.where(own_seen, scores_of(query, own), lowest_score)
        new_scores = jnp.where(new_seen, scores_of(query, new), lowest_score)
        maxima = jnp.maximum(
            jnp.max(own_scores, axis=1, keepdims=True), jnp.max(new_scores, axis=1, keepdims=True)
        )
        own_exp = jnp.exp2(own_scores * log2_scale - maxima * log2_scale)
        new_exp = jnp.exp2(new_scores * log2_scale - maxima * log2_scale)
        sums = jnp.sum(own_exp, axis=1, keepdims=True) + jnp.sum(new_exp, axis=1, keepdims=True)
        acc_ref[at, :] = jnp.dot(
            own_exp.astype(jnp.bfloat16), own[:, :rank_dim], preferred_element_type=jnp.float32
        ) + jnp.dot(
            new_exp.astype(jnp.bfloat16), new[:, :rank_dim], preferred_element_type=jnp.float32
        )
        write_stats(stats_ref, at, maxima, sums)


def prompt_kernel(block, rows_per_request, half, rank_dim, finish, lens_ref, route_ref, query_ref,
                  keys_ref, places_ref):
    count = query_ref.shape[0] // block
    key_count = keys_ref.shape[0]
    per_block = block // rows_per_request
    active = route_ref[0] > 0
    places = places_ref[half * 8 : (half + 1) * 8, :]
    scores = scores_of(query_ref[0:block, :], keys_ref[...])
    for number in range(count):
        at = slice(number * block, (number + 1) * block)
        following = None
        if number + 1 < count:
            following = scores_of(
                query_ref[(number + 1) * block : (number + 2) * block, :], keys_ref[...]
            )
        parts = []
        for request in range(per_block):
            seen = places < jnp.where(active, lens_ref[number * per_block + request], 0)
            part = scores[request * rows_per_request : (request + 1) * rows_per_request]
            part = part.reshape(rows_per_request // 8, 8, key_count)
            part = jnp.where(seen[None], part, lowest_score)
            parts.append(part.reshape(rows_per_request, key_count))
        scores = jnp.concatenate(parts, axis=0)
        maxima = jnp.max(scores, axis=1, keepdims=True)
        expons = jnp.exp2(scores * log2_scale - maxima * log2_scale)
        sums = jnp.sum(expons, axis=1, keepdims=True)
        weighted = jnp.dot(
            expons.astype(jnp.bfloat16), keys_ref[:, :rank_dim],
            preferred_element_type=jnp.float32,
        )
        finish(number, at, maxima, sums, weighted)
        scores = following


def first_kernel(block, rows_per_request, lens_ref, route_ref, query_ref, keys_ref, places_ref,
                 stats_ref, acc_ref):

    def keep(number, at, maxima, sums, weighted):
        acc_ref[at, :] = weighted
        write_stats(stats_ref, at, maxima, sums)

    prompt_kernel(
        block, rows_per_request, 0, acc_ref.shape[1], keep, lens_ref, route_ref, query_ref,
        keys_ref, places_ref,
    )


def last_kernel(block, rows_per_request, heads, lens_ref, route_ref, query_ref, keys_ref,
                places_ref, stats_ref, acc_ref, local_stats_ref, local_ref, uv_ref, out_ref,
                latent_ref):
    def divide(number, at, maxima, sums, weighted):
        first_max, first_sums = read_stats(stats_ref, at)
        local_max, local_sums = read_stats(local_stats_ref, at)
        peak = jnp.maximum(jnp.maximum(maxima, first_max), local_max)
        factor = jnp.exp2((maxima - peak) * log2_scale)
        first_factor = jnp.exp2((first_max - peak) * log2_scale)
        local_factor = jnp.exp2((local_max - peak) * log2_scale)
        inverse = 1.0 / (sums * factor + first_sums * first_factor + local_sums * local_factor)
        latent = (
            weighted * (factor * inverse)
            + acc_ref[at, :] * (first_factor * inverse)
            + local_ref[at, :] * (local_factor * inverse)
        )
        latent = latent.astype(jnp.bfloat16).astype(jnp.float32)
        for part in range(latent_ref.shape[0]):
            latent_ref[part, at, :] = latent[:, part * 128 : (part + 1) * 128]

    prompt_kernel(
        block, rows_per_request, 1, acc_ref.shape[1], divide, lens_ref, route_ref, query_ref,
        keys_ref, places_ref,
    )
    requests, steps = out_ref.shape[:2]
    vhead = uv_ref.shape[2]
    for head in range(heads):
        rows = jnp.concatenate(
            [
                latent_ref[part, pl.ds(head, requests * steps, stride=heads), :].astype(jnp.bfloat16)
                for part in range(latent_ref.shape[0])
            ],
            axis=1,
        )
        product = jnp.dot(rows, uv_ref[head], preferred_element_type=jnp.float32)
        out_ref[:, :, head * vhead : (head + 1) * vhead] = product.reshape(
            requests, steps, vhead
        ).astype(jnp.bfloat16)


def body(
    queries, new_latent, own_cache, prompt_pool, uv_weight, owner, route, prompt_len, page_table
):
    requests, num_steps, head_dev, latent = queries.shape
    rank_dim = uv_weight.shape[1]
    vhead_dim = uv_weight.shape[2]
    num_pages = page_table.shape[0]
    own_pages, page_len = prompt_pool.shape[1:3]
    row_count = requests * num_steps * head_dev
    rows_per_request = num_steps * head_dev
    query_rows = queries.reshape(row_count, latent)

    group_ids = jnp.arange(owner.shape[0], dtype=jnp.int32)
    root = jnp.sum(jnp.where(owner == 0, group_ids, 0))
    root_high = root // 8
    root_piece = root % 8

    pieces = prompt_pool.reshape(8, own_pages * page_len // 8, latent)
    pieces = lax.all_to_all(pieces, ("y", "c"), 0, 0, tiled=True)
    piece = lax.dynamic_index_in_dim(pieces, root_piece, 0, keepdims=False)
    piece = lax.switch(root_high, [functools.partial(from_high, high) for high in range(4)], piece)
    run = gathered(piece, "zl", 4)
    half = gathered(run.reshape(-1, latent), ("x", "y"), 16)
    block = 256
    vmem = pl.BlockSpec(memory_space=pltpu.VMEM)
    smem = pl.BlockSpec(memory_space=pltpu.SMEM)
    params = pltpu.CompilerParams(vmem_limit_bytes=12 * 1024 * 1024)
    stats_shape = [
        jax.ShapeDtypeStruct((row_count, 128), jnp.float32),
        jax.ShapeDtypeStruct((row_count, rank_dim), jnp.float32),
    ]
    key_count = num_pages * page_len // 2
    local = pl.pallas_call(
        functools.partial(
            local_kernel, head_dev, num_steps, block, page_len, own_pages * page_len // 8
        ),
        in_specs=[smem] + [vmem] * 3,
        out_specs=[vmem] * 3,
        out_shape=stats_shape + [jax.ShapeDtypeStruct((16, key_count), jnp.int32)],
        compiler_params=params,
        cost_estimate=pl.CostEstimate(
            flops=2 * row_count * block * (latent + rank_dim) * 2,
            bytes_accessed=8 * row_count * rank_dim,
            transcendentals=row_count * block,
        ),
    )
    stats, acc, places = local(
        page_table, query_rows, own_cache.reshape(-1, latent), new_latent.reshape(-1, latent)
    )
    half, stats, acc, places = lax.optimization_barrier((half, stats, acc, places))
    other = lax.ppermute(half, "c", [(0, 1), (1, 0)]).reshape(-1, latent)
    half = half.reshape(-1, latent)
    cost = pl.CostEstimate(
        flops=2 * row_count * key_count * (latent + rank_dim),
        bytes_accessed=2 * (row_count + key_count) * latent + 4 * row_count * rank_dim,
        transcendentals=row_count * key_count,
    )
    wide = pltpu.CompilerParams(vmem_limit_bytes=20 * 1024 * 1024)
    first = pl.pallas_call(
        functools.partial(first_kernel, block, rows_per_request),
        in_specs=[smem, smem] + [vmem] * 3,
        out_specs=[vmem] * 2,
        out_shape=stats_shape,
        compiler_params=wide,
        cost_estimate=cost,
    )
    first_stats, first_acc = first(prompt_len, route, query_rows, half, places)
    last = pl.pallas_call(
        functools.partial(last_kernel, block, rows_per_request, head_dev),
        in_specs=[smem, smem] + [vmem] * 8,
        out_specs=vmem,
        scratch_shapes=[pltpu.VMEM((rank_dim // 128, row_count, 128), jnp.float32)],
        out_shape=jax.ShapeDtypeStruct((requests, num_steps, head_dev * vhead_dim), jnp.bfloat16),
        compiler_params=wide,
        cost_estimate=cost,
    )
    return last(
        prompt_len, route, query_rows, other, places, first_stats, first_acc, stats, acc, uv_weight
    )


def solution(mesh):
    fine = Mesh(mesh.devices.reshape(axis_sizes), axis_names)
    placed = (
        P(group_axes, None, head_axes, None),
        P(group_axes, None, None),
        P(group_axes, None, None),
        P(group_axes, head_axes, None, None),
        P(head_axes, None, None),
        P(),
        P(group_axes),
        P(group_axes),
        P(),
    )
    return jax.shard_map(
        body, mesh=fine, in_specs=placed, out_specs=P(group_axes, None, head_axes), check_vma=False
    )
```

```python
import functools

import jax
import jax.numpy as jnp
from jax import lax
from jax.experimental import pallas as pl
from jax.experimental.pallas import tpu as pltpu
from jax.sharding import Mesh, PartitionSpec as P

softmax_scale = 192.0 ** (-0.5)
lowest_score = -1e30
log2_scale = softmax_scale * 1.4426950408889634

axis_names = ("zh", "y", "c", "x", "zl")
axis_sizes = (4, 4, 2, 4, 4)
group_axes = ("zh", "y", "c")
head_axes = ("x", "zl")


def from_high(high, piece):
    place = lax.axis_index("zh")
    up, down, across = (high + 1) % 4, (high + 3) % 4, (high + 2) % 4
    above = lax.ppermute(piece, "zh", [(high, up)])
    below = lax.ppermute(piece, "zh", [(high, down)])
    beyond = lax.ppermute(above, "zh", [(up, across)])
    result = jnp.where(place == up, above, piece)
    result = jnp.where(place == down, below, result)
    return jnp.where(place == across, beyond, result)


def gathered(value, axes, count):
    tiled = jnp.broadcast_to(value[None], (count,) + value.shape)
    return lax.all_to_all(tiled, axes, 0, 0, tiled=True)


def scores_of(query, keys):
    return lax.dot_general(
        query, keys, (((1,), (1,)), ((), ())), preferred_element_type=jnp.float32
    )


def read_stats(stats_ref, at):
    return stats_ref[at, 0:1], stats_ref[at, 1:2]


def write_stats(stats_ref, at, maxima, sums):
    rows = maxima.shape[0]
    lane = lax.broadcasted_iota(jnp.int32, (rows, stats_ref.shape[1]), 1)
    stats_ref[at, :] = jnp.where(lane == 0, maxima, sums)


def write_places(page_len, piece_rows, table_ref, places_ref):
    shape = (8, places_ref.shape[1])
    lane = lax.broadcasted_iota(jnp.int32, shape, 1)
    low = lane // piece_rows % 4
    lower = lane // (piece_rows * 4) % 2
    page = lane // (piece_rows * 8) % 2
    slot = (lane // (piece_rows * 16) * 4 + low) * 2 + page
    places = lower * (2 * piece_rows) + lane % piece_rows
    for logical in range(table_ref.shape[0]):
        places += jnp.where(slot == table_ref[logical], logical * page_len, 0)
    core = lax.axis_index("c")
    places_ref[0:8, :] = places + core * piece_rows
    places_ref[8:16, :] = places + (1 - core) * piece_rows


def local_kernel(heads, steps, block, page_len, piece_rows, table_ref, query_ref, own_ref, new_ref,
                 stats_ref, acc_ref, places_ref):
    write_places(page_len, piece_rows, table_ref, places_ref)
    rows = query_ref.shape[0]
    rank_dim = acc_ref.shape[1]
    requests = rows // (heads * steps)
    own_len = own_ref.shape[0] // requests
    tokens = block // heads
    per_block = tokens // steps
    row = lax.broadcasted_iota(jnp.int32, (block, per_block * own_len), 0) % tokens
    key = lax.broadcasted_iota(jnp.int32, (block, per_block * own_len), 1)
    own_seen = row // steps == key // own_len
    row = lax.broadcasted_iota(jnp.int32, (block, tokens), 0) % tokens
    key = lax.broadcasted_iota(jnp.int32, (block, tokens), 1)
    new_seen = (row // steps == key // steps) & (key <= row)
    for number in range(rows // block):
        at = slice(number * block, (number + 1) * block)
        query = query_ref[at, :]
        own = own_ref[number * per_block * own_len : (number + 1) * per_block * own_len, :]
        new = new_ref[number * tokens : (number + 1) * tokens, :]
        own_scores = jnp.where(own_seen, scores_of(query, own), lowest_score)
        new_scores = jnp.where(new_seen, scores_of(query, new), lowest_score)
        maxima = jnp.maximum(
            jnp.max(own_scores, axis=1, keepdims=True), jnp.max(new_scores, axis=1, keepdims=True)
        )
        own_exp = jnp.exp2(own_scores * log2_scale - maxima * log2_scale)
        new_exp = jnp.exp2(new_scores * log2_scale - maxima * log2_scale)
        sums = jnp.sum(own_exp, axis=1, keepdims=True) + jnp.sum(new_exp, axis=1, keepdims=True)
        acc_ref[at, :] = jnp.dot(
            own_exp.astype(jnp.bfloat16), own[:, :rank_dim], preferred_element_type=jnp.float32
        ) + jnp.dot(
            new_exp.astype(jnp.bfloat16), new[:, :rank_dim], preferred_element_type=jnp.float32
        )
        write_stats(stats_ref, at, maxima, sums)


def prompt_kernel(block, heads, steps, half, rank_dim, finish, lens_ref, query_ref,
                  keys_ref, places_ref):
    count = query_ref.shape[0] // block
    tokens = block // heads
    key_count = keys_ref.shape[0]
    places = places_ref[half * 8 : (half + 1) * 8, :]
    sublane = lax.broadcasted_iota(jnp.int32, places.shape, 0)
    scores = scores_of(query_ref[0:block, :], keys_ref[...])
    for number in range(count):
        at = slice(number * block, (number + 1) * block)
        following = None
        if number + 1 < count:
            following = scores_of(
                query_ref[(number + 1) * block : (number + 2) * block, :], keys_ref[...]
            )
        scores = scores.reshape(heads, tokens // 8, 8, key_count)
        parts = []
        for pair in range(tokens // 8):
            request = (number * tokens + pair * 8) // steps
            limit = jnp.where(sublane < steps, lens_ref[request], lens_ref[request + 1])
            parts.append(jnp.where((places < limit)[None], scores[:, pair], lowest_score))
        scores = jnp.stack(parts, axis=1).reshape(block, key_count)
        maxima = jnp.max(scores, axis=1, keepdims=True)
        expons = jnp.exp2(scores * log2_scale - maxima * log2_scale)
        sums = jnp.sum(expons, axis=1, keepdims=True)
        weighted = jnp.dot(
            expons.astype(jnp.bfloat16), keys_ref[:, :rank_dim],
            preferred_element_type=jnp.float32,
        )
        finish(number, at, maxima, sums, weighted)
        scores = following


def first_kernel(block, heads, steps, lens_ref, query_ref, keys_ref, places_ref,
                 stats_ref, acc_ref):
    def keep(number, at, maxima, sums, weighted):
        acc_ref[at, :] = weighted
        write_stats(stats_ref, at, maxima, sums)

    prompt_kernel(
        block, heads, steps, 0, acc_ref.shape[1], keep, lens_ref, query_ref,
        keys_ref, places_ref,
    )


def last_kernel(block, heads, lens_ref, query_ref, keys_ref, places_ref,
                stats_ref, acc_ref, local_stats_ref, local_ref, uv_ref, out_ref, latent_ref):
    requests, steps = out_ref.shape[:2]
    tokens = block // heads

    def divide(number, at, maxima, sums, weighted):
        first_max, first_sums = read_stats(stats_ref, at)
        local_max, local_sums = read_stats(local_stats_ref, at)
        peak = jnp.maximum(jnp.maximum(maxima, first_max), local_max)
        factor = jnp.exp2((maxima - peak) * log2_scale)
        first_factor = jnp.exp2((first_max - peak) * log2_scale)
        local_factor = jnp.exp2((local_max - peak) * log2_scale)
        inverse = 1.0 / (sums * factor + first_sums * first_factor + local_sums * local_factor)
        latent = (
            weighted * (factor * inverse)
            + acc_ref[at, :] * (first_factor * inverse)
            + local_ref[at, :] * (local_factor * inverse)
        ).astype(jnp.bfloat16)
        for head in range(heads):
            latent_ref[head, number * tokens : (number + 1) * tokens, :] = latent[
                head * tokens : (head + 1) * tokens
            ]

    prompt_kernel(
        block, heads, steps, 1, acc_ref.shape[1], divide, lens_ref, query_ref,
        keys_ref, places_ref,
    )
    vhead = uv_ref.shape[2]
    for head in range(heads):
        product = jnp.dot(latent_ref[head], uv_ref[head], preferred_element_type=jnp.float32)
        out_ref[:, :, head * vhead : (head + 1) * vhead] = product.reshape(
            requests, steps, vhead
        ).astype(jnp.bfloat16)


def body(
    queries, new_latent, own_cache, prompt_pool, uv_weight, owner, route, prompt_len, page_table
):
    requests, num_steps, head_dev, latent = queries.shape
    rank_dim = uv_weight.shape[1]
    vhead_dim = uv_weight.shape[2]
    num_pages = page_table.shape[0]
    own_pages, page_len = prompt_pool.shape[1:3]
    row_count = requests * num_steps * head_dev
    block = 256
    tokens = block // head_dev
    query_rows = queries.reshape(-1, tokens, head_dev, latent).transpose(0, 2, 1, 3)
    query_rows = query_rows.reshape(row_count, latent)

    group_ids = jnp.arange(owner.shape[0], dtype=jnp.int32)
    root = jnp.sum(jnp.where(owner == 0, group_ids, 0))
    root_high = jnp.right_shift(root, 3)
    root_piece = jnp.bitwise_and(root, 7)

    pieces = prompt_pool.reshape(8, own_pages * page_len // 8, latent)
    pieces = lax.all_to_all(pieces, ("y", "c"), 0, 0, tiled=True)
    piece = lax.dynamic_index_in_dim(
        pieces, root_piece, 0, keepdims=False, allow_negative_indices=False
    )
    piece = lax.switch(root_high, [functools.partial(from_high, high) for high in range(4)], piece)
    run = gathered(piece, "zl", 4).reshape(-1, latent)
    half = gathered(run, ("x", "y"), 16)

    vmem = pl.BlockSpec(memory_space=pltpu.VMEM)
    smem = pl.BlockSpec(memory_space=pltpu.SMEM)
    params = pltpu.CompilerParams(vmem_limit_bytes=12 * 1024 * 1024)
    stats_shape = [
        jax.ShapeDtypeStruct((row_count, 128), jnp.float32),
        jax.ShapeDtypeStruct((row_count, rank_dim), jnp.float32),
    ]
    key_count = num_pages * page_len // 2
    local = pl.pallas_call(
        functools.partial(
            local_kernel, head_dev, num_steps, block, page_len, own_pages * page_len // 8
        ),
        in_specs=[smem] + [vmem] * 3,
        out_specs=[vmem] * 3,
        out_shape=stats_shape + [jax.ShapeDtypeStruct((16, key_count), jnp.int32)],
        compiler_params=params,
        cost_estimate=pl.CostEstimate(
            flops=2 * row_count * block * (latent + rank_dim) * 2,
            bytes_accessed=8 * row_count * rank_dim,
            transcendentals=row_count * block,
        ),
    )
    stats, acc, places = local(
        page_table, query_rows, own_cache.reshape(-1, latent), new_latent.reshape(-1, latent)
    )
    lens = jnp.where(route[0] > 0, prompt_len, 0)
    half, stats, acc, places, lens = lax.optimization_barrier((half, stats, acc, places, lens))
    other = lax.ppermute(half, "c", [(0, 1), (1, 0)]).reshape(-1, latent)
    half = half.reshape(-1, latent)
    cost = pl.CostEstimate(
        flops=2 * row_count * key_count * (latent + rank_dim),
        bytes_accessed=2 * (row_count + key_count) * latent + 4 * row_count * rank_dim,
        transcendentals=row_count * key_count,
    )
    wide = pltpu.CompilerParams(vmem_limit_bytes=20 * 1024 * 1024)
    first = pl.pallas_call(
        functools.partial(first_kernel, block, head_dev, num_steps),
        in_specs=[smem] + [vmem] * 3,
        out_specs=[vmem] * 2,
        out_shape=stats_shape,
        compiler_params=wide,
        cost_estimate=cost,
    )
    first_stats, first_acc = first(lens, query_rows, half, places)
    last = pl.pallas_call(
        functools.partial(last_kernel, block, head_dev),
        in_specs=[smem] + [vmem] * 8,
        out_specs=vmem,
        scratch_shapes=[pltpu.VMEM((head_dev, requests * num_steps, rank_dim), jnp.bfloat16)],
        out_shape=jax.ShapeDtypeStruct((requests, num_steps, head_dev * vhead_dim), jnp.bfloat16),
        compiler_params=wide,
        cost_estimate=cost,
    )
    return last(
        lens, query_rows, other, places, first_stats, first_acc, stats, acc,
        uv_weight,
    )


def solution(mesh):
    fine = Mesh(mesh.devices.reshape(axis_sizes), axis_names)
    placed = (
        P(group_axes, None, head_axes, None),
        P(group_axes, None, None),
        P(group_axes, None, None),
        P(group_axes, head_axes, None, None),
        P(head_axes, None, None),
        P(),
        P(group_axes),
        P(group_axes),
        P(),
    )
    return jax.shard_map(
        body, mesh=fine, in_specs=placed, out_specs=P(group_axes, None, head_axes), check_vma=False
    )
```

```python
import functools

import jax
import jax.numpy as jnp
from jax import lax
from jax.experimental import pallas as pl
from jax.experimental.pallas import tpu as pltpu
from jax.sharding import Mesh, PartitionSpec as P

softmax_scale = 192.0 ** (-0.5)
lowest_score = -1e30
log2_scale = softmax_scale * 1.4426950408889634

axis_names = ("zh", "y", "c", "x", "zl")
axis_sizes = (4, 4, 2, 4, 4)
group_axes = ("zh", "y", "c")
head_axes = ("x", "zl")


def from_high(high, piece):
    place = lax.axis_index("zh")
    up, down, across = (high + 1) % 4, (high + 3) % 4, (high + 2) % 4
    above = lax.ppermute(piece, "zh", [(high, up)])
    held = jnp.where(place == up, above, piece)
    onward = lax.ppermute(held, "zh", [(high, down), (up, across)])
    return jnp.where((place == down) | (place == across), onward, held)


def gathered(value, axes, count):
    tiled = jnp.broadcast_to(value[None], (count,) + value.shape)
    return lax.all_to_all(tiled, axes, 0, 0, tiled=True)


def scores_of(query, keys):
    return lax.dot_general(
        query, keys, (((1,), (1,)), ((), ())), preferred_element_type=jnp.float32
    )


def read_stats(stats_ref, at):
    return stats_ref[at, 0:1], stats_ref[at, 1:2]


def write_stats(stats_ref, at, maxima, sums):
    rows = maxima.shape[0]
    lane = lax.broadcasted_iota(jnp.int32, (rows, stats_ref.shape[1]), 1)
    stats_ref[at, :] = jnp.where(lane == 0, maxima, sums)


def write_places(page_len, piece_rows, table_ref, places_ref):
    shape = (8, places_ref.shape[1])
    lane = lax.broadcasted_iota(jnp.int32, shape, 1)
    low = lane // piece_rows % 4
    lower = lane // (piece_rows * 4) % 2
    page = lane // (piece_rows * 8) % 2
    slot = (lane // (piece_rows * 16) * 4 + low) * 2 + page
    places = lower * (2 * piece_rows) + lane % piece_rows
    for logical in range(table_ref.shape[0]):
        places += jnp.where(slot == table_ref[logical], logical * page_len, 0)
    core = lax.axis_index("c")
    places_ref[0:8, :] = places + core * piece_rows
    places_ref[8:16, :] = places + (1 - core) * piece_rows


def local_kernel(heads, steps, block, page_len, piece_rows, table_ref, query_ref, own_ref, new_ref,
                 stats_ref, acc_ref, places_ref):
    write_places(page_len, piece_rows, table_ref, places_ref)
    rows = query_ref.shape[0]
    rank_dim = acc_ref.shape[1]
    requests = rows // (heads * steps)
    own_len = own_ref.shape[0] // requests
    tokens = block // heads
    per_block = tokens // steps
    row = lax.broadcasted_iota(jnp.int32, (block, per_block * own_len), 0) % tokens
    key = lax.broadcasted_iota(jnp.int32, (block, per_block * own_len), 1)
    own_seen = row // steps == key // own_len
    row = lax.broadcasted_iota(jnp.int32, (block, tokens), 0) % tokens
    key = lax.broadcasted_iota(jnp.int32, (block, tokens), 1)
    new_seen = (row // steps == key // steps) & (key <= row)
    for number in range(rows // block):
        at = slice(number * block, (number + 1) * block)
        query = query_ref[at, :]
        own = own_ref[number * per_block * own_len : (number + 1) * per_block * own_len, :]
        new = new_ref[number * tokens : (number + 1) * tokens, :]
        own_scores = jnp.where(own_seen, scores_of(query, own), lowest_score)
        new_scores = jnp.where(new_seen, scores_of(query, new), lowest_score)
        maxima = jnp.maximum(
            jnp.max(own_scores, axis=1, keepdims=True), jnp.max(new_scores, axis=1, keepdims=True)
        )
        own_exp = jnp.exp2(own_scores * log2_scale - maxima * log2_scale)
        new_exp = jnp.exp2(new_scores * log2_scale - maxima * log2_scale)
        sums = jnp.sum(own_exp, axis=1, keepdims=True) + jnp.sum(new_exp, axis=1, keepdims=True)
        acc_ref[at, :] = jnp.dot(
            own_exp.astype(jnp.bfloat16), own[:, :rank_dim], preferred_element_type=jnp.float32
        ) + jnp.dot(
            new_exp.astype(jnp.bfloat16), new[:, :rank_dim], preferred_element_type=jnp.float32
        )
        write_stats(stats_ref, at, maxima, sums)


def prompt_kernel(block, heads, steps, half, rank_dim, finish, lens_ref, query_ref,
                  keys_ref, places_ref):
    count = query_ref.shape[0] // block
    tokens = block // heads
    key_count = keys_ref.shape[0]
    places = places_ref[half * 8 : (half + 1) * 8, :]
    sublane = lax.broadcasted_iota(jnp.int32, places.shape, 0)
    scores = scores_of(query_ref[0:block, :], keys_ref[...])
    for number in range(count):
        at = slice(number * block, (number + 1) * block)
        following = None
        if number + 1 < count:
            following = scores_of(
                query_ref[(number + 1) * block : (number + 2) * block, :], keys_ref[...]
            )
        scores = scores.reshape(heads, tokens // 8, 8, key_count)
        parts = []
        for pair in range(tokens // 8):
            request = (number * tokens + pair * 8) // steps
            limit = jnp.where(sublane < steps, lens_ref[request], lens_ref[request + 1])
            parts.append(jnp.where((places < limit)[None], scores[:, pair], lowest_score))
        scores = jnp.stack(parts, axis=1).reshape(block, key_count)
        maxima = jnp.max(scores, axis=1, keepdims=True)
        expons = jnp.exp2(scores * log2_scale - maxima * log2_scale)
        sums = jnp.sum(expons, axis=1, keepdims=True)
        weighted = jnp.dot(
            expons.astype(jnp.bfloat16), keys_ref[:, :rank_dim],
            preferred_element_type=jnp.float32,
        )
        finish(number, at, maxima, sums, weighted)
        scores = following


def first_kernel(block, heads, steps, lens_ref, query_ref, keys_ref, places_ref,
                 stats_ref, acc_ref):
    def keep(number, at, maxima, sums, weighted):
        acc_ref[at, :] = weighted
        write_stats(stats_ref, at, maxima, sums)

    prompt_kernel(
        block, heads, steps, 0, acc_ref.shape[1], keep, lens_ref, query_ref,
        keys_ref, places_ref,
    )


def last_kernel(block, heads, lens_ref, query_ref, keys_ref, places_ref,
                stats_ref, acc_ref, local_stats_ref, local_ref, uv_ref, out_ref, latent_ref):
    requests, steps = out_ref.shape[:2]
    tokens = block // heads

    def divide(number, at, maxima, sums, weighted):
        first_max, first_sums = read_stats(stats_ref, at)
        local_max, local_sums = read_stats(local_stats_ref, at)
        peak = jnp.maximum(jnp.maximum(maxima, first_max), local_max)
        factor = jnp.exp2((maxima - peak) * log2_scale)
        first_factor = jnp.exp2((first_max - peak) * log2_scale)
        local_factor = jnp.exp2((local_max - peak) * log2_scale)
        inverse = 1.0 / (sums * factor + first_sums * first_factor + local_sums * local_factor)
        latent = (
            weighted * (factor * inverse)
            + acc_ref[at, :] * (first_factor * inverse)
            + local_ref[at, :] * (local_factor * inverse)
        ).astype(jnp.bfloat16)
        for head in range(heads):
            latent_ref[head, number * tokens : (number + 1) * tokens, :] = latent[
                head * tokens : (head + 1) * tokens
            ]

    prompt_kernel(
        block, heads, steps, 1, acc_ref.shape[1], divide, lens_ref, query_ref,
        keys_ref, places_ref,
    )
    vhead = uv_ref.shape[2]
    for head in range(heads):
        product = jnp.dot(latent_ref[head], uv_ref[head], preferred_element_type=jnp.float32)
        out_ref[:, :, head * vhead : (head + 1) * vhead] = product.reshape(
            requests, steps, vhead
        ).astype(jnp.bfloat16)


def body(
    queries, new_latent, own_cache, prompt_pool, uv_weight, owner, route, prompt_len, page_table
):
    requests, num_steps, head_dev, latent = queries.shape
    rank_dim = uv_weight.shape[1]
    vhead_dim = uv_weight.shape[2]
    num_pages = page_table.shape[0]
    own_pages, page_len = prompt_pool.shape[1:3]
    row_count = requests * num_steps * head_dev
    block = 256
    tokens = block // head_dev
    query_rows = queries.reshape(-1, tokens, head_dev, latent).transpose(0, 2, 1, 3)
    query_rows = query_rows.reshape(row_count, latent)

    group_ids = jnp.arange(owner.shape[0], dtype=jnp.int32)
    root = jnp.sum(jnp.where(owner == 0, group_ids, 0))
    root_high = jnp.right_shift(root, 3)
    root_piece = jnp.bitwise_and(root, 7)

    pieces = prompt_pool.reshape(8, own_pages * page_len // 8, latent)
    pieces = lax.all_to_all(pieces, ("y", "c"), 0, 0, tiled=True)
    piece = lax.dynamic_index_in_dim(
        pieces, root_piece, 0, keepdims=False, allow_negative_indices=False
    )
    piece = lax.switch(root_high, [functools.partial(from_high, high) for high in range(4)], piece)
    run = gathered(piece, "zl", 4).reshape(-1, latent)
    half = gathered(run, ("x", "y"), 16)

    vmem = pl.BlockSpec(memory_space=pltpu.VMEM)
    smem = pl.BlockSpec(memory_space=pltpu.SMEM)
    params = pltpu.CompilerParams(vmem_limit_bytes=12 * 1024 * 1024)
    stats_shape = [
        jax.ShapeDtypeStruct((row_count, 128), jnp.float32),
        jax.ShapeDtypeStruct((row_count, rank_dim), jnp.float32),
    ]
    key_count = num_pages * page_len // 2
    local = pl.pallas_call(
        functools.partial(
            local_kernel, head_dev, num_steps, block, page_len, own_pages * page_len // 8
        ),
        in_specs=[smem] + [vmem] * 3,
        out_specs=[vmem] * 3,
        out_shape=stats_shape + [jax.ShapeDtypeStruct((16, key_count), jnp.int32)],
        compiler_params=params,
        cost_estimate=pl.CostEstimate(
            flops=2 * row_count * block * (latent + rank_dim) * 2,
            bytes_accessed=8 * row_count * rank_dim,
            transcendentals=row_count * block,
        ),
    )
    stats, acc, places = local(
        page_table, query_rows, own_cache.reshape(-1, latent), new_latent.reshape(-1, latent)
    )
    lens = jnp.where(route[0] > 0, prompt_len, 0)
    half, stats, acc, places, lens = lax.optimization_barrier((half, stats, acc, places, lens))
    other = lax.ppermute(half, "c", [(0, 1), (1, 0)]).reshape(-1, latent)
    half = half.reshape(-1, latent)
    cost = pl.CostEstimate(
        flops=2 * row_count * key_count * (latent + rank_dim),
        bytes_accessed=2 * (row_count + key_count) * latent + 4 * row_count * rank_dim,
        transcendentals=row_count * key_count,
    )
    wide = pltpu.CompilerParams(vmem_limit_bytes=20 * 1024 * 1024)
    first = pl.pallas_call(
        functools.partial(first_kernel, block, head_dev, num_steps),
        in_specs=[smem] + [vmem] * 3,
        out_specs=[vmem] * 2,
        out_shape=stats_shape,
        compiler_params=wide,
        cost_estimate=cost,
    )
    first_stats, first_acc = first(lens, query_rows, half, places)
    last = pl.pallas_call(
        functools.partial(last_kernel, block, head_dev),
        in_specs=[smem] + [vmem] * 8,
        out_specs=vmem,
        scratch_shapes=[pltpu.VMEM((head_dev, requests * num_steps, rank_dim), jnp.bfloat16)],
        out_shape=jax.ShapeDtypeStruct((requests, num_steps, head_dev * vhead_dim), jnp.bfloat16),
        compiler_params=wide,
        cost_estimate=cost,
    )
    return last(
        lens, query_rows, other, places, first_stats, first_acc, stats, acc,
        uv_weight,
    )


def solution(mesh):
    fine = Mesh(mesh.devices.reshape(axis_sizes), axis_names)
    placed = (
        P(group_axes, None, head_axes, None),
        P(group_axes, None, None),
        P(group_axes, None, None),
        P(group_axes, head_axes, None, None),
        P(head_axes, None, None),
        P(),
        P(group_axes),
        P(group_axes),
        P(),
    )
    return jax.shard_map(
        body, mesh=fine, in_specs=placed, out_specs=P(group_axes, None, head_axes), check_vma=False
    )
```
